32 devices in a mesh: grp: 2 (over y), ep: 8 (over z, x), sub: 2 (over core).
Axes of the slice: x: 2, y: 2, z: 4, core: 2. Of those that a mesh axis runs over, the one named last changes fastest.
Arguments:
- tokens: bfloat16 [2, 16, 3584], P(None, ('grp', 'ep'), 'sub'), parts along dimension 1, may hold values from -6 to 6
- route_experts: int32 [2, 16, 8], P(None, 'grp'), parts along dimension 1, may hold values from 0 to 15, all different within a row; in each aligned block of 8 rows (0 to 7, 8 to 15, ..., all dimensions but the last counted through in order) at most 6 rows name the same one
- route_weight: float32 [2, 16, 8], P(None, 'grp'), parts along dimension 1, may hold values from 0.05 to 0.6
- expert_slot: int32 [16], replicated, may hold values from 0 to 15, each once
- w_gate: bfloat16 [3584, 32768], P(None, ('ep', 'sub')), may hold values from -0.09375 to 0.09375
- w_up: bfloat16 [3584, 32768], P(None, ('ep', 'sub')), may hold values from -0.09375 to 0.09375
- w_down: bfloat16 [32768, 3584], P(('ep', 'sub')), may hold values from -0.125 to 0.125
Outputs:
- mixed: bfloat16 [2, 16, 3584], P(None, ('grp', 'ep'), 'sub'), parts along dimension 1
The draws below stay inside these ranges and needn't reach their ends.
There are 2 independent parts, one for each index of `grp`. The reference program is written for one: setup_inputs(seed, part) draws one part's arguments, and reference() takes and returns one part's arrays. A program takes and returns all parts, laid end to end along the dimension named above; an argument that names none is the same for every part. Nothing has to cross between parts.
Inputs may be any that keep to these rules, and one draw needn't show every extreme that they name: `route_experts`: in each step no expert is chosen by more than 6 of the 8 tokens, a bound that some block reaches; a token's 8 experts differ. `expert_slot`: each slot holds exactly one expert.
All inputs are finite; a program needn't handle non-finite values.
Results may differ from the reference program's by a relative error of at most 0.005.
Values may be sent and summed in bfloat16 or wider, within the bound.
A program may use at most 128 MiB of HBM per device.

```python
import math
import jax
import jax.numpy as jnp
import numpy as np
from jax import lax

D = 3584
FF = 2048
EXPERTS = 16
TOP = 8
STEPS = 2
TOKENS = 8
MOST = 6


def level_of(rng, extent, shards, smallest, largest):
    gain = 1.0
    for dim, parts in shards:
        draws = jax.random.uniform(jax.random.fold_in(jax.random.fold_in(rng, 6), dim), (parts,), jnp.float32, smallest / len(shards), largest / len(shards))
        gain = gain * jnp.repeat(jnp.exp(draws), extent[dim] // parts).reshape((-1,) + (1,) * (len(extent) - 1 - dim))
    return gain


def assign_block(rng, own, number, rows, count, top, most, skew):
    sequence = jax.random.permutation(rng, count)
    heavy_load, common = portions_of(count, rows * top, most, skew, True), portions_of(count, rows * top, most, skew, False)
    places = jnp.arange(count)

    def named(sizes, rotation):
        used = int((sizes > 0).sum())
        fixed = max(1, used // 4)
        shifted = fixed + (places - fixed + rotation * (used - fixed)) % max(1, count - fixed)
        return jnp.zeros((count,), jnp.int32).at[sequence[jnp.where(places < fixed, places, shifted)]].set(jnp.asarray(sizes, jnp.int32))

    sizes = jnp.where(number % 4 == 0, named(heavy_load, number // 4), named(common, number - number // 4 - 1))
    mixed = jax.random.permutation(jax.random.fold_in(own, 3), count)
    source_of, receiver = mixed[0:count // 2 * 2:2], mixed[1:count // 2 * 2:2]
    room = jnp.minimum(sizes[source_of] - 1, most - sizes[receiver]) // 2
    room = jnp.where((source_of == sequence[0]) | (receiver == sequence[0]) | (sizes[receiver] == 0), 0, jnp.maximum(room, 0))
    shifted = jax.random.randint(jax.random.fold_in(own, 4), (count // 2,), 0, 1 << 20) % (room + 1)
    sizes = sizes.at[source_of].add(-shifted).at[receiver].add(shifted)
    members = jnp.searchsorted(jnp.cumsum(sizes), jnp.arange(rows * top), side="right").astype(jnp.int32)
    listing = members.reshape(top, rows).T
    listing = listing[jax.random.permutation(jax.random.fold_in(own, 1), rows)]
    rotation = jax.random.randint(jax.random.fold_in(own, 2), (rows, 1), 0, top)
    return jnp.take_along_axis(listing, (jnp.arange(top)[None, :] + rotation) % top, axis=1)


def portions_of(number_of, total, most, slope, full):
    portions = [(1 << 20) // math.isqrt(rank ** slope) + 1 for rank in range(1, number_of + 1)]
    largest = most if full else min(most, max(-(-total // number_of), total * portions[0] // sum(portions)))
    least = 1 if total - largest >= number_of - 1 else 0
    holding, spare = [largest] + [least] * (number_of - 1), total - largest - least * (number_of - 1)
    while spare > 0:
        free = [i for i in range(1, number_of) if holding[i] < largest] or [i for i in range(1, number_of) if holding[i] < most]
        mass, left = sum([portions[i] for i in free]), spare
        for i in free:
            addition = min(most - holding[i], max(1, left * portions[i] // mass), spare)
            holding[i] = holding[i] + addition
            spare = spare - addition
    return np.array(holding)


def centred(stream_key, dims, spread, most, split=(), kind=jnp.bfloat16):
    factor_of = level_of(stream_key, dims, split, -0.22, 0.18) if split else 1.0
    result = jax.random.normal(stream_key, dims, jnp.float32) * spread * factor_of
    return jnp.minimum(jnp.maximum(result, -most), most).astype(kind)


def setup_inputs(seed: int = 0, part: int = 0) -> dict:
    arg_keys = jax.random.split(jax.random.key(seed), 8)
    part_keys = jax.random.split(jax.random.fold_in(arg_keys[7], part), 8)
    tokens = centred(part_keys[0], (STEPS, TOKENS, D), 1.0, 6.0, ((1, 8), (2, 2)))
    route_experts_keys = jax.random.split(jax.random.fold_in(part_keys[1], 1), STEPS * TOKENS // TOKENS)
    route_experts_turns = jax.random.permutation(jax.random.fold_in(part_keys[1], 3), STEPS * TOKENS // TOKENS)
    route_experts = jax.vmap(lambda own, number: assign_block(jax.random.fold_in(part_keys[1], 2), own, number, TOKENS, EXPERTS, TOP, MOST, 2))(route_experts_keys, route_experts_turns).reshape((STEPS, TOKENS, TOP))
    route_weight = jnp.clip(jnp.exp(jax.random.uniform(part_keys[2], (STEPS, TOKENS, TOP), jnp.float32, math.log(0.05), math.log(0.6))), 0.05, 0.6)
    expert_slot = jax.random.permutation(arg_keys[3], EXPERTS).astype(jnp.int32)
    w_gate = centred(arg_keys[4], (D, EXPERTS * FF), D ** -0.5, 0.09375, ((1, 16),))
    w_up = centred(arg_keys[5], (D, EXPERTS * FF), D ** -0.5, 0.09375, ((1, 16),))
    w_down = centred(arg_keys[6], (EXPERTS * FF, D), FF ** -0.5, 0.125, ((0, 16),))
    return {"tokens": tokens, "route_experts": route_experts, "route_weight": route_weight, "expert_slot": expert_slot, "w_gate": w_gate, "w_up": w_up, "w_down": w_down}


def reference(tokens, route_experts, route_weight, expert_slot, w_gate, w_up, w_down):
    labels = jnp.arange(EXPERTS, dtype=jnp.int32)
    results = []
    for step in range(STEPS):
        rows = tokens[step]
        chosen_experts = route_experts[step]
        chosen_weight = route_weight[step]

        def one_expert(total, expert):
            slot = jnp.sum(jnp.where(labels == expert, expert_slot, 0)).astype(jnp.int32)
            scale = jnp.sum(jnp.where(chosen_experts == expert, chosen_weight, 0.0), axis=1)
            start = (slot * FF).astype(jnp.int32)
            gate_cols = lax.dynamic_slice_in_dim(w_gate, start, FF, 1)
            up_cols = lax.dynamic_slice_in_dim(w_up, start, FF, 1)
            down_rows = lax.dynamic_slice_in_dim(w_down, start, FF, 0)
            gate = jnp.dot(rows, gate_cols, preferred_element_type=jnp.float32)
            up = jnp.dot(rows, up_cols, preferred_element_type=jnp.float32)
            hidden = (jax.nn.silu(gate) * up).astype(jnp.bfloat16)
            part = jnp.dot(hidden, down_rows, preferred_element_type=jnp.float32)
            return total + scale[:, None] * part, None

        total, unused = lax.scan(one_expert, jnp.zeros((TOKENS, D), jnp.float32), labels)
        results.append(total.astype(jnp.bfloat16))
    return jnp.stack(results)
```

```python
import jax
import jax.numpy as jnp
from jax import lax
from jax.experimental import pallas as pl
from jax.experimental.pallas import tpu as pltpu
from jax.sharding import PartitionSpec as P

FF = 2048
LANES = 128
BLOCK = 256
MESH = pl.DeviceIdType.MESH


def swiglu(rows, gate_cols, up_cols, down_rows):
    gate = jnp.dot(rows, gate_cols, preferred_element_type=jnp.float32)
    up = jnp.dot(rows, up_cols, preferred_element_type=jnp.float32)
    hidden = (jax.nn.silu(gate) * up).astype(jnp.bfloat16)
    return jnp.dot(hidden, down_rows, preferred_element_type=jnp.float32)


def expert_terms(rows, experts, weights, expert_slot, w_gate, w_up, w_down, first_col):
    labels = jnp.arange(expert_slot.shape[0], dtype=jnp.int32)
    slot = (first_col + 0) // FF
    logical = jnp.sum(jnp.where(expert_slot == slot, labels, 0))
    chosen = experts == logical
    scale = jnp.sum(jnp.where(chosen, weights, 0.0), axis=1)
    total = scale[:, None] * swiglu(rows, w_gate, w_up, w_down)
    return total


def collect(local):
    gathered = lax.all_gather(local, "ep", axis=0, tiled=True)
    return lax.all_gather(gathered, "sub", axis=1, tiled=True)


def spread(total):
    owned = lax.psum_scatter(total, "ep", scatter_dimension=0, tiled=True)
    return lax.psum_scatter(owned, "sub", scatter_dimension=1, tiled=True)


def with_collectives(tokens, route_experts, route_weight, expert_slot, w_gate, w_up, w_down):
    sub_size = lax.axis_size("sub")
    first_col = (lax.axis_index("ep") * sub_size + lax.axis_index("sub")) * w_gate.shape[1]
    steps, count, part = tokens.shape
    rows = jnp.stack([collect(tokens[step]) for step in range(steps)])
    results = []
    for step in range(steps):
        total = expert_terms(
            rows[step],
            route_experts[step],
            route_weight[step],
            expert_slot,
            w_gate,
            w_up,
            w_down,
            first_col,
        )
        results.append(spread(total).astype(jnp.bfloat16))
    return jnp.stack(results)


def layer_kernel(
    peers,
    sub_size,
    slots_ref,
    tokens_ref,
    experts_ref,
    weights_ref,
    gate_ref,
    up_ref,
    down_ref,
    out_ref,
    tok,
    exp_in,
    wt_in,
    stage,
    mine,
    gathered,
    wide,
    rows,
    gates,
    ups,
    downs,
    hidden,
    spreadout,
    sendbuf,
    landed,
    small_sem,
    gate_sem,
    up_sem,
    down_sem,
    tok_send,
    tok_recv,
    sum_send,
    sum_recv,
):
    steps, _, part = tokens_ref.shape
    ep_size = peers // sub_size
    pad = stage.shape[0] // steps
    cols = part // LANES
    n_up = gates.shape[0]
    n_half = part // BLOCK
    grp = lax.axis_index("grp")
    my_ep = lax.axis_index("ep")
    my_sub = lax.axis_index("sub")
    me = my_ep * sub_size + my_sub

    barrier = pltpu.get_barrier_semaphore()

    def greet(o, carry):
        peer = lax.rem(me + o, peers)
        pl.semaphore_signal(
            barrier,
            inc=1,
            device_id=(grp, peer // sub_size, lax.rem(peer, sub_size)),
            device_id_type=MESH,
        )
        return carry

    lax.fori_loop(1, peers, greet, 0)

    small = [
        pltpu.make_async_copy(tokens_ref, tok, small_sem.at[0]),
        pltpu.make_async_copy(experts_ref, exp_in, small_sem.at[1]),
        pltpu.make_async_copy(weights_ref, wt_in, small_sem.at[2]),
    ]
    for copy in small:
        copy.start()

    def gate_copy(c):
        at = pl.multiple_of(c * BLOCK, BLOCK)
        return pltpu.make_async_copy(gate_ref.at[:, pl.ds(at, BLOCK)], gates.at[c], gate_sem.at[c])

    def up_copy(c):
        at = pl.multiple_of(c * BLOCK, BLOCK)
        return pltpu.make_async_copy(up_ref.at[:, pl.ds(at, BLOCK)], ups.at[c], up_sem.at[c])

    def down_copy(c):
        at = pl.multiple_of(c * BLOCK, BLOCK)
        return pltpu.make_async_copy(down_ref.at[:, pl.ds(at, BLOCK)], downs.at[c], down_sem.at[c])

    def start_up(c, carry):
        gate_copy(c).start()
        up_copy(c).start()
        return carry

    def start_down(c, carry):
        down_copy(c).start()
        return carry

    lax.fori_loop(0, n_up, start_up, 0)
    lax.fori_loop(0, downs.shape[0], start_down, 0)

    for copy in small:
        copy.wait()
    stage[...] = jnp.zeros_like(stage)
    for t in range(steps):
        row = tok[t].astype(jnp.float32)
        for c in range(cols):
            stage[t * pad + c : t * pad + c + 1, :] = row[:, c * LANES : (c + 1) * LANES]
    mine[...] = stage[...].astype(jnp.bfloat16)
    gathered[me] = mine[...]

    pl.semaphore_wait(barrier, peers - 1)

    def token_copy(peer, slot):
        return pltpu.make_async_remote_copy(
            src_ref=mine,
            dst_ref=gathered.at[slot],
            send_sem=tok_send.at[peer],
            recv_sem=tok_recv.at[slot],
            device_id=(grp, peer // sub_size, lax.rem(peer, sub_size)),
            device_id_type=MESH,
        )

    def send_tokens(o, carry):
        token_copy(lax.rem(me + o, peers), me).start()
        return carry

    lax.fori_loop(1, peers, send_tokens, 0)

    logical = jnp.int32(0)
    for e in range(slots_ref.shape[0]):
        logical += jnp.where(slots_ref[e] == me, jnp.int32(e), jnp.int32(0))
    scales = [
        jnp.sum(
            jnp.where(exp_in[t] == logical, wt_in[t], 0.0), axis=1, keepdims=True
        )
        for t in range(steps)
    ]

    def land_tokens(o, carry):
        peer = lax.rem(me + o, peers)
        token_copy(peer, peer).wait_recv()
        return carry

    lax.fori_loop(1, peers, land_tokens, 0)
    wide[...] = gathered[...].astype(jnp.float32).reshape(wide.shape)
    for s in range(sub_size):
        for c in range(cols):
            picked = [
                wide[pl.ds(s * steps * pad + t * pad + c, ep_size, stride=sub_size * steps * pad), :]
                for t in range(steps)
            ]
            at = s * part + c * LANES
            rows[:, at : at + LANES] = jnp.concatenate(picked, axis=0).astype(jnp.bfloat16)

    def hide(c, carry):
        gate_copy(c).wait()
        up_copy(c).wait()
        gate = jnp.dot(rows[...], gates[c], preferred_element_type=jnp.float32)
        up = jnp.dot(rows[...], ups[c], preferred_element_type=jnp.float32)
        value = gate / (1.0 + jnp.exp(-gate)) * up
        hidden[:, pl.ds(pl.multiple_of(c * BLOCK, BLOCK), BLOCK)] = value.astype(jnp.bfloat16)
        return carry

    lax.fori_loop(0, n_up, hide, 0)

    spreadout[...] = jnp.zeros_like(spreadout)

    def sum_copy(owner, slot):
        return pltpu.make_async_remote_copy(
            src_ref=sendbuf.at[owner],
            dst_ref=landed.at[slot],
            send_sem=sum_send.at[owner],
            recv_sem=sum_recv.at[slot],
            device_id=(grp, owner // sub_size, lax.rem(owner, sub_size)),
            device_id_type=MESH,
        )

    for s in range(sub_size):

        def lower(n, carry):
            down_copy(s * n_half + n).wait()
            value = jnp.dot(hidden[...], downs[s * n_half + n], preferred_element_type=jnp.float32)
            for t in range(steps):
                term = value[t * ep_size : (t + 1) * ep_size] * scales[t]
                for k in range(BLOCK // LANES):
                    start = t * pad + n * (BLOCK // LANES) + k
                    spreadout[pl.ds(start, ep_size, stride=steps * pad), :] = term[
                        :, k * LANES : (k + 1) * LANES
                    ]
            return carry

        lax.fori_loop(0, n_half, lower, 0)

        def send_sums(o, carry):
            j = lax.rem(my_ep + o, ep_size)
            owner = j * sub_size + s
            first = pl.multiple_of(j * steps * pad, steps * pad)
            block = spreadout[pl.ds(first, steps * pad), :].astype(jnp.bfloat16)

            @pl.when(owner == me)
            def _():
                landed[me] = block

            @pl.when(owner != me)
            def _():
                sendbuf[owner] = block
                sum_copy(owner, me).start()

            return carry

        lax.fori_loop(1, ep_size + 1, send_sums, 0)

    def land_sums(o, carry):
        peer = lax.rem(me + o, peers)
        sum_copy(peer, peer).wait_recv()
        return carry

    lax.fori_loop(1, peers, land_sums, 0)
    total = landed[0].astype(jnp.float32)
    for p in range(1, peers):
        total += landed[p].astype(jnp.float32)
    out_ref[...] = total.astype(jnp.bfloat16)

    def sent(o, carry):
        peer = lax.rem(me + o, peers)
        token_copy(peer, me).wait_send()
        sum_copy(peer, me).wait_send()
        return carry

    lax.fori_loop(1, peers, sent, 0)


def with_kernel(tokens, route_experts, route_weight, expert_slot, w_gate, w_up, w_down):
    sub_size = lax.axis_size("sub")
    ep_size = lax.axis_size("ep")
    peers = sub_size * ep_size
    steps, _, part = tokens.shape
    depth, width = w_gate.shape
    cols = part // LANES
    pad = -(-cols // 16) * 16
    block = steps * pad
    bf16, f32 = jnp.bfloat16, jnp.float32
    dma = pltpu.SemaphoreType.DMA

    def body(*refs):
        layer_kernel(peers, sub_size, *refs)

    out = pl.pallas_call(
        body,
        out_shape=jax.ShapeDtypeStruct((block, LANES), bf16),
        in_specs=[pl.BlockSpec(memory_space=pltpu.SMEM)] + [pl.BlockSpec(memory_space=pl.ANY)] * 6,
        out_specs=pl.BlockSpec(memory_space=pltpu.VMEM),
        scratch_shapes=[
            pltpu.VMEM(tokens.shape, bf16),
            pltpu.VMEM(route_experts.shape, jnp.int32),
            pltpu.VMEM(route_weight.shape, f32),
            pltpu.VMEM((block, LANES), f32),
            pltpu.VMEM((block, LANES), bf16),
            pltpu.VMEM((peers, block, LANES), bf16),
            pltpu.VMEM((peers * block, LANES), f32),
            pltpu.VMEM((steps * ep_size, depth), bf16),
            pltpu.VMEM((width // BLOCK, depth, BLOCK), bf16),
            pltpu.VMEM((width // BLOCK, depth, BLOCK), bf16),
            pltpu.VMEM((depth // BLOCK, width, BLOCK), bf16),
            pltpu.VMEM((steps * ep_size, width), bf16),
            pltpu.VMEM((ep_size * block, LANES), f32),
            pltpu.VMEM((peers, block, LANES), bf16),
            pltpu.VMEM((peers, block, LANES), bf16),
            dma((3,)),
            dma((width // BLOCK,)),
            dma((width // BLOCK,)),
            dma((depth // BLOCK,)),
            dma((peers,)),
            dma((peers,)),
            dma((peers,)),
            dma((peers,)),
        ],
        compiler_params=pltpu.CompilerParams(
            collective_id=0, has_side_effects=True, vmem_limit_bytes=56 * 1024 * 1024
        ),
        cost_estimate=pl.CostEstimate(
            flops=6 * steps * ep_size * depth * width,
            bytes_accessed=6 * depth * width,
            transcendentals=steps * ep_size * width,
        ),
    )(expert_slot, tokens, route_experts, route_weight, w_gate, w_up, w_down)
    return out.reshape(steps, pad, LANES)[:, :cols].reshape(steps, 1, part)


def on_device(tokens, route_experts, route_weight, expert_slot, w_gate, w_up, w_down):
    fits = (
        w_gate.shape[1] == FF
        and tokens.shape[1] == 1
        and tokens.shape[2] % BLOCK == 0
        and lax.axis_size("ep") == 8
    )
    plan = with_kernel if fits else with_collectives
    return plan(tokens, route_experts, route_weight, expert_slot, w_gate, w_up, w_down)


def solution(mesh):
    return jax.shard_map(
        on_device,
        mesh=mesh,
        in_specs=(
            P(None, ("grp", "ep"), "sub"),
            P(None, "grp", None),
            P(None, "grp", None),
            P(),
            P(None, ("ep", "sub")),
            P(None, ("ep", "sub")),
            P(("ep", "sub"), None),
        ),
        out_specs=P(None, ("grp", "ep"), "sub"),
        check_vma=False,
    )
```

```python
import jax
import jax.numpy as jnp
from jax import lax
from jax.experimental import pallas as pl
from jax.experimental.pallas import tpu as pltpu
from jax.sharding import PartitionSpec as P

FF = 2048
LANES = 128
UP_BLOCK = 512
DOWN_BLOCK = 1792
MESH = pl.DeviceIdType.MESH


def swiglu(rows, gate_cols, up_cols, down_rows):
    gate = jnp.dot(rows, gate_cols, preferred_element_type=jnp.float32)
    up = jnp.dot(rows, up_cols, preferred_element_type=jnp.float32)
    hidden = (jax.nn.silu(gate) * up).astype(jnp.bfloat16)
    return jnp.dot(hidden, down_rows, preferred_element_type=jnp.float32)


def expert_terms(rows, experts, weights, expert_slot, w_gate, w_up, w_down, first_col):
    labels = jnp.arange(expert_slot.shape[0], dtype=jnp.int32)
    slot = (first_col + 0) // FF
    logical = jnp.sum(jnp.where(expert_slot == slot, labels, 0))
    chosen = experts == logical
    scale = jnp.sum(jnp.where(chosen, weights, 0.0), axis=1)
    total = scale[:, None] * swiglu(rows, w_gate, w_up, w_down)
    return total


def collect(local):
    gathered = lax.all_gather(local, "ep", axis=0, tiled=True)
    return lax.all_gather(gathered, "sub", axis=1, tiled=True)


def spread(total):
    owned = lax.psum_scatter(total, "ep", scatter_dimension=0, tiled=True)
    return lax.psum_scatter(owned, "sub", scatter_dimension=1, tiled=True)


def with_collectives(tokens, route_experts, route_weight, expert_slot, w_gate, w_up, w_down):
    sub_size = lax.axis_size("sub")
    first_col = (lax.axis_index("ep") * sub_size + lax.axis_index("sub")) * w_gate.shape[1]
    steps, count, part = tokens.shape
    rows = jnp.stack([collect(tokens[step]) for step in range(steps)])
    results = []
    for step in range(steps):
        total = expert_terms(
            rows[step],
            route_experts[step],
            route_weight[step],
            expert_slot,
            w_gate,
            w_up,
            w_down,
            first_col,
        )
        results.append(spread(total).astype(jnp.bfloat16))
    return jnp.stack(results)


def layer_kernel(
    peers,
    sub_size,
    slots_ref,
    tokens_ref,
    experts_ref,
    weights_ref,
    gate_ref,
    up_ref,
    down_ref,
    out_ref,
    slots,
    tok,
    exp_in,
    wt_in,
    stage,
    mine,
    gathered,
    wide,
    rows,
    gates,
    ups,
    downs,
    hidden,
    spreadout,
    sendbuf,
    landed,
    small_sem,
    gate_sem,
    up_sem,
    down_sem,
    tok_send,
    tok_recv,
    sum_send,
    sum_recv,
):
    steps, part = tokens_ref.shape
    ep_size = peers // sub_size
    pad = stage.shape[0] // steps
    cols = part // LANES
    n_up = gates.shape[0]
    n_half = part // DOWN_BLOCK
    grp = lax.axis_index("grp")
    my_ep = lax.axis_index("ep")
    my_sub = lax.axis_index("sub")
    me = my_ep * sub_size + my_sub

    barrier = pltpu.get_barrier_semaphore()

    def greet(o, carry):
        peer = lax.rem(me + o, peers)
        pl.semaphore_signal(
            barrier,
            inc=1,
            device_id=(grp, peer // sub_size, lax.rem(peer, sub_size)),
            device_id_type=MESH,
        )
        return carry

    lax.fori_loop(1, peers, greet, 0)

    small = [
        pltpu.make_async_copy(tokens_ref, tok, small_sem.at[0]),
        pltpu.make_async_copy(experts_ref, exp_in, small_sem.at[1]),
        pltpu.make_async_copy(weights_ref, wt_in, small_sem.at[2]),
        pltpu.make_async_copy(slots_ref, slots, small_sem.at[3]),
    ]
    for copy in small:
        copy.start()

    def gate_copy(c):
        at = pl.multiple_of(c * UP_BLOCK, UP_BLOCK)
        return pltpu.make_async_copy(gate_ref.at[:, pl.ds(at, UP_BLOCK)], gates.at[c], gate_sem.at[c])

    def up_copy(c):
        at = pl.multiple_of(c * UP_BLOCK, UP_BLOCK)
        return pltpu.make_async_copy(up_ref.at[:, pl.ds(at, UP_BLOCK)], ups.at[c], up_sem.at[c])

    def down_copy(c):
        at = pl.multiple_of(c * DOWN_BLOCK, DOWN_BLOCK)
        return pltpu.make_async_copy(down_ref.at[:, pl.ds(at, DOWN_BLOCK)], downs.at[c], down_sem.at[c])

    def start_up(c, carry):
        gate_copy(c).start()
        up_copy(c).start()
        return carry

    def start_down(c, carry):
        down_copy(c).start()
        return carry

    lax.fori_loop(0, n_up, start_up, 0)
    lax.fori_loop(0, downs.shape[0], start_down, 0)

    stage[...] = jnp.zeros_like(stage)
    small[0].wait()
    for t in range(steps):
        row = tok[t : t + 1, :].astype(jnp.float32)
        for c in range(cols):
            stage[t * pad + c : t * pad + c + 1, :] = row[:, c * LANES : (c + 1) * LANES]
    mine[...] = stage[...].astype(jnp.bfloat16)
    gathered[me] = mine[...]

    pl.semaphore_wait(barrier, peers - 1)

    def token_copy(peer, slot):
        return pltpu.make_async_remote_copy(
            src_ref=mine,
            dst_ref=gathered.at[slot],
            send_sem=tok_send.at[peer],
            recv_sem=tok_recv.at[slot],
            device_id=(grp, peer // sub_size, lax.rem(peer, sub_size)),
            device_id_type=MESH,
        )

    def send_tokens(o, carry):
        token_copy(lax.rem(me + o, peers), me).start()
        return carry

    lax.fori_loop(1, peers, send_tokens, 0)

    spreadout[...] = jnp.zeros_like(spreadout)
    for copy in small[1:]:
        copy.wait()

    logical = jnp.int32(0)
    for e in range(slots.shape[0]):
        logical += jnp.where(slots[e] == me, jnp.int32(e), jnp.int32(0))
    scales = [
        jnp.sum(
            jnp.where(exp_in[t] == logical, wt_in[t], 0.0), axis=1, keepdims=True
        )
        for t in range(steps)
    ]

    def land_tokens(o, carry):
        peer = lax.rem(me + o, peers)
        token_copy(peer, peer).wait_recv()
        return carry

    lax.fori_loop(1, peers, land_tokens, 0)
    wide[...] = gathered[...].astype(jnp.float32).reshape(wide.shape)
    for s in range(sub_size):
        for c in range(cols):
            picked = [
                wide[pl.ds(s * steps * pad + t * pad + c, ep_size, stride=sub_size * steps * pad), :]
                for t in range(steps)
            ]
            at = s * part + c * LANES
            rows[:, at : at + LANES] = jnp.concatenate(picked, axis=0).astype(jnp.bfloat16)

    def hide(c, carry):
        gate_copy(c).wait()
        up_copy(c).wait()
        gate = jnp.dot(rows[...], gates[c], preferred_element_type=jnp.float32)
        up = jnp.dot(rows[...], ups[c], preferred_element_type=jnp.float32)
        value = gate / (1.0 + jnp.exp(-gate)) * up
        hidden[:, pl.ds(pl.multiple_of(c * UP_BLOCK, UP_BLOCK), UP_BLOCK)] = value.astype(jnp.bfloat16)
        return carry

    lax.fori_loop(0, n_up, hide, 0)

    def sum_copy(owner, slot):
        return pltpu.make_async_remote_copy(
            src_ref=sendbuf.at[owner],
            dst_ref=landed.at[slot],
            send_sem=sum_send.at[owner],
            recv_sem=sum_recv.at[slot],
            device_id=(grp, owner // sub_size, lax.rem(owner, sub_size)),
            device_id_type=MESH,
        )

    for s in range(sub_size):

        def lower(n, carry):
            down_copy(s * n_half + n).wait()
            value = jnp.dot(hidden[...], downs[s * n_half + n], preferred_element_type=jnp.float32)
            for t in range(steps):
                term = value[t * ep_size : (t + 1) * ep_size] * scales[t]
                for k in range(DOWN_BLOCK // LANES):
                    start = t * pad + n * (DOWN_BLOCK // LANES) + k
                    spreadout[pl.ds(start, ep_size, stride=steps * pad), :] = term[
                        :, k * LANES : (k + 1) * LANES
                    ]
            return carry

        lax.fori_loop(0, n_half, lower, 0)

        def send_sums(o, carry):
            j = lax.rem(my_ep + o, ep_size)
            owner = j * sub_size + s
            first = pl.multiple_of(j * steps * pad, steps * pad)
            block = spreadout[pl.ds(first, steps * pad), :].astype(jnp.bfloat16)

            @pl.when(owner == me)
            def _():
                landed[me] = block

            @pl.when(owner != me)
            def _():
                sendbuf[owner] = block
                sum_copy(owner, me).start()

            return carry

        lax.fori_loop(1, ep_size + 1, send_sums, 0)

    def land_sums(o, carry):
        peer = lax.rem(me + o, peers)
        sum_copy(peer, peer).wait_recv()
        return carry

    lax.fori_loop(1, peers, land_sums, 0)
    total = landed[0].astype(jnp.float32)
    for p in range(1, peers):
        total += landed[p].astype(jnp.float32)
    for t in range(steps):
        at = t * pad
        row = jnp.concatenate([total[at + c : at + c + 1] for c in range(cols)], axis=1)
        out_ref[t : t + 1, :] = row.astype(jnp.bfloat16)

    def sent(o, carry):
        peer = lax.rem(me + o, peers)
        token_copy(peer, me).wait_send()
        sum_copy(peer, me).wait_send()
        return carry

    lax.fori_loop(1, peers, sent, 0)


def with_kernel(tokens, route_experts, route_weight, expert_slot, w_gate, w_up, w_down):
    sub_size = lax.axis_size("sub")
    ep_size = lax.axis_size("ep")
    peers = sub_size * ep_size
    steps, _, part = tokens.shape
    depth, width = w_gate.shape
    cols = part // LANES
    pad = -(-cols // 16) * 16
    block = steps * pad
    bf16, f32 = jnp.bfloat16, jnp.float32
    dma = pltpu.SemaphoreType.DMA

    def body(*refs):
        layer_kernel(peers, sub_size, *refs)

    out = pl.pallas_call(
        body,
        out_shape=jax.ShapeDtypeStruct((steps, part), bf16),
        in_specs=[pl.BlockSpec(memory_space=pl.ANY)] * 7,
        out_specs=pl.BlockSpec(memory_space=pltpu.VMEM),
        scratch_shapes=[
            pltpu.SMEM(expert_slot.shape, jnp.int32),
            pltpu.VMEM((steps, part), bf16),
            pltpu.VMEM(route_experts.shape, jnp.int32),
            pltpu.VMEM(route_weight.shape, f32),
            pltpu.VMEM((block, LANES), f32),
            pltpu.VMEM((block, LANES), bf16),
            pltpu.VMEM((peers, block, LANES), bf16),
            pltpu.VMEM((peers * block, LANES), f32),
            pltpu.VMEM((steps * ep_size, depth), bf16),
            pltpu.VMEM((width // UP_BLOCK, depth, UP_BLOCK), bf16),
            pltpu.VMEM((width // UP_BLOCK, depth, UP_BLOCK), bf16),
            pltpu.VMEM((depth // DOWN_BLOCK, width, DOWN_BLOCK), bf16),
            pltpu.VMEM((steps * ep_size, width), bf16),
            pltpu.VMEM((ep_size * block, LANES), f32),
            pltpu.VMEM((peers, block, LANES), bf16),
            pltpu.VMEM((peers, block, LANES), bf16),
            dma((4,)),
            dma((width // UP_BLOCK,)),
            dma((width // UP_BLOCK,)),
            dma((depth // DOWN_BLOCK,)),
            dma((peers,)),
            dma((peers,)),
            dma((peers,)),
            dma((peers,)),
        ],
        compiler_params=pltpu.CompilerParams(
            collective_id=0, has_side_effects=True, vmem_limit_bytes=56 * 1024 * 1024
        ),
        cost_estimate=pl.CostEstimate(
            flops=6 * steps * ep_size * depth * width,
            bytes_accessed=6 * depth * width,
            transcendentals=steps * ep_size * width,
        ),
    )(expert_slot, tokens.reshape(steps, part), route_experts, route_weight, w_gate, w_up, w_down)
    return out.reshape(steps, 1, part)


def on_device(tokens, route_experts, route_weight, expert_slot, w_gate, w_up, w_down):
    fits = (
        w_gate.shape[1] == FF
        and tokens.shape[1] == 1
        and tokens.shape[2] % DOWN_BLOCK == 0
        and lax.axis_size("ep") == 8
    )
    plan = with_kernel if fits else with_collectives
    return plan(tokens, route_experts, route_weight, expert_slot, w_gate, w_up, w_down)


def solution(mesh):
    return jax.shard_map(
        on_device,
        mesh=mesh,
        in_specs=(
            P(None, ("grp", "ep"), "sub"),
            P(None, "grp", None),
            P(None, "grp", None),
            P(),
            P(None, ("ep", "sub")),
            P(None, ("ep", "sub")),
            P(("ep", "sub"), None),
        ),
        out_specs=P(None, ("grp", "ep"), "sub"),
        check_vma=False,
    )
```

```python
import jax
import jax.numpy as jnp
from jax import lax
from jax.experimental import pallas as pl
from jax.experimental.pallas import tpu as pltpu
from jax.sharding import PartitionSpec as P

FF = 2048
LANES = 128
UP_BLOCK = 1024
DOWN_BLOCK = 1792
MESH = pl.DeviceIdType.MESH


def swiglu(rows, gate_cols, up_cols, down_rows):
    gate = jnp.dot(rows, gate_cols, preferred_element_type=jnp.float32)
    up = jnp.dot(rows, up_cols, preferred_element_type=jnp.float32)
    hidden = (jax.nn.silu(gate) * up).astype(jnp.bfloat16)
    return jnp.dot(hidden, down_rows, preferred_element_type=jnp.float32)


def expert_terms(rows, experts, weights, expert_slot, w_gate, w_up, w_down, first_col):
    labels = jnp.arange(expert_slot.shape[0], dtype=jnp.int32)
    slot = (first_col + 0) // FF
    logical = jnp.sum(jnp.where(expert_slot == slot, labels, 0))
    chosen = experts == logical
    scale = jnp.sum(jnp.where(chosen, weights, 0.0), axis=1)
    total = scale[:, None] * swiglu(rows, w_gate, w_up, w_down)
    return total


def collect(local):
    gathered = lax.all_gather(local, "ep", axis=0, tiled=True)
    return lax.all_gather(gathered, "sub", axis=1, tiled=True)


def spread(total):
    owned = lax.psum_scatter(total, "ep", scatter_dimension=0, tiled=True)
    return lax.psum_scatter(owned, "sub", scatter_dimension=1, tiled=True)


def with_collectives(tokens, route_experts, route_weight, expert_slot, w_gate, w_up, w_down):
    sub_size = lax.axis_size("sub")
    first_col = (lax.axis_index("ep") * sub_size + lax.axis_index("sub")) * w_gate.shape[1]
    steps, count, part = tokens.shape
    rows = jnp.stack([collect(tokens[step]) for step in range(steps)])
    results = []
    for step in range(steps):
        total = expert_terms(
            rows[step],
            route_experts[step],
            route_weight[step],
            expert_slot,
            w_gate,
            w_up,
            w_down,
            first_col,
        )
        results.append(spread(total).astype(jnp.bfloat16))
    return jnp.stack(results)


def layer_kernel(
    peers,
    sub_size,
    slots_ref,
    tokens_ref,
    experts_ref,
    weights_ref,
    gate_ref,
    up_ref,
    down_ref,
    out_ref,
    slots,
    tok,
    exp_in,
    wt_in,
    stage,
    mine,
    gathered,
    wide,
    rows,
    gates,
    ups,
    downs,
    hidden,
    spreadout,
    sendbuf,
    landed,
    small_sem,
    gate_sem,
    up_sem,
    down_sem,
    tok_send,
    tok_recv,
    sum_send,
    sum_recv,
):
    steps, part = tokens_ref.shape
    ep_size = peers // sub_size
    pad = stage.shape[0] // steps
    cols = part // LANES
    n_up = gates.shape[0]
    n_half = part // DOWN_BLOCK
    grp = lax.axis_index("grp")
    my_ep = lax.axis_index("ep")
    my_sub = lax.axis_index("sub")
    me = my_ep * sub_size + my_sub

    barrier = pltpu.get_barrier_semaphore()

    def greet(o, carry):
        peer = lax.rem(me + o, peers)
        pl.semaphore_signal(
            barrier,
            inc=1,
            device_id=(grp, peer // sub_size, lax.rem(peer, sub_size)),
            device_id_type=MESH,
        )
        return carry

    lax.fori_loop(1, peers, greet, 0, unroll=True)

    small = [
        pltpu.make_async_copy(tokens_ref, tok, small_sem.at[0]),
        pltpu.make_async_copy(experts_ref, exp_in, small_sem.at[1]),
        pltpu.make_async_copy(weights_ref, wt_in, small_sem.at[2]),
        pltpu.make_async_copy(slots_ref, slots, small_sem.at[3]),
    ]
    for copy in small:
        copy.start()

    def gate_copy(c):
        at = pl.multiple_of(c * UP_BLOCK, UP_BLOCK)
        return pltpu.make_async_copy(gate_ref.at[:, pl.ds(at, UP_BLOCK)], gates.at[c], gate_sem.at[c])

    def up_copy(c):
        at = pl.multiple_of(c * UP_BLOCK, UP_BLOCK)
        return pltpu.make_async_copy(up_ref.at[:, pl.ds(at, UP_BLOCK)], ups.at[c], up_sem.at[c])

    def down_copy(c):
        at = pl.multiple_of(c * DOWN_BLOCK, DOWN_BLOCK)
        return pltpu.make_async_copy(down_ref.at[:, pl.ds(at, DOWN_BLOCK)], downs.at[c], down_sem.at[c])

    def start_up(c, carry):
        gate_copy(c).start()
        up_copy(c).start()
        return carry

    def start_down(c, carry):
        down_copy(c).start()
        return carry

    lax.fori_loop(0, n_up, start_up, 0, unroll=True)
    lax.fori_loop(0, downs.shape[0], start_down, 0)

    stage[...] = jnp.zeros_like(stage)
    small[0].wait()
    for t in range(steps):
        row = tok[t : t + 1, :].astype(jnp.float32)
        for c in range(cols):
            stage[t * pad + c : t * pad + c + 1, :] = row[:, c * LANES : (c + 1) * LANES]
    mine[...] = stage[...].astype(jnp.bfloat16)
    gathered[me] = mine[...]

    pl.semaphore_wait(barrier, peers - 1)

    def token_copy(peer, slot):
        return pltpu.make_async_remote_copy(
            src_ref=mine,
            dst_ref=gathered.at[slot],
            send_sem=tok_send.at[peer],
            recv_sem=tok_recv.at[slot],
            device_id=(grp, peer // sub_size, lax.rem(peer, sub_size)),
            device_id_type=MESH,
        )

    def send_tokens(o, carry):
        token_copy(lax.rem(me + o, peers), me).start()
        return carry

    lax.fori_loop(1, peers, send_tokens, 0, unroll=True)

    spreadout[...] = jnp.zeros_like(spreadout)
    for copy in small[1:]:
        copy.wait()

    logical = jnp.int32(0)
    for e in range(slots.shape[0]):
        logical += jnp.where(slots[e] == me, jnp.int32(e), jnp.int32(0))
    scales = [
        jnp.sum(
            jnp.where(exp_in[t] == logical, wt_in[t], 0.0), axis=1, keepdims=True
        )
        for t in range(steps)
    ]

    def land_tokens(o, carry):
        peer = lax.rem(me + o, peers)
        token_copy(peer, peer).wait_recv()
        return carry

    lax.fori_loop(1, peers, land_tokens, 0, unroll=True)
    wide[...] = gathered[...].astype(jnp.float32).reshape(wide.shape)
    for s in range(sub_size):
        for c in range(cols):
            picked = [
                wide[pl.ds(s * steps * pad + t * pad + c, ep_size, stride=sub_size * steps * pad), :]
                for t in range(steps)
            ]
            at = s * part + c * LANES
            rows[:, at : at + LANES] = jnp.concatenate(picked, axis=0).astype(jnp.bfloat16)

    def hide(c, carry):
        gate_copy(c).wait()
        up_copy(c).wait()
        gate = jnp.dot(rows[...], gates[c], preferred_element_type=jnp.float32)
        up = jnp.dot(rows[...], ups[c], preferred_element_type=jnp.float32)
        value = gate / (1.0 + jnp.exp(-gate)) * up
        hidden[:, pl.ds(pl.multiple_of(c * UP_BLOCK, UP_BLOCK), UP_BLOCK)] = value.astype(jnp.bfloat16)
        return carry

    lax.fori_loop(0, n_up, hide, 0, unroll=True)

    def sum_copy(owner, slot):
        return pltpu.make_async_remote_copy(
            src_ref=sendbuf.at[owner],
            dst_ref=landed.at[slot],
            send_sem=sum_send.at[owner],
            recv_sem=sum_recv.at[slot],
            device_id=(grp, owner // sub_size, lax.rem(owner, sub_size)),
            device_id_type=MESH,
        )

    for s in range(sub_size):

        def lower(n, carry):
            down_copy(s * n_half + n).wait()
            value = jnp.dot(hidden[...], downs[s * n_half + n], preferred_element_type=jnp.float32)
            for t in range(steps):
                term = value[t * ep_size : (t + 1) * ep_size] * scales[t]
                for k in range(DOWN_BLOCK // LANES):
                    start = t * pad + n * (DOWN_BLOCK // LANES) + k
                    spreadout[pl.ds(start, ep_size, stride=steps * pad), :] = term[
                        :, k * LANES : (k + 1) * LANES
                    ]
            return carry

        lax.fori_loop(0, n_half, lower, 0)

        def send_sums(o, carry):
            j = lax.rem(my_ep + o, ep_size)
            owner = j * sub_size + s
            first = pl.multiple_of(j * steps * pad, steps * pad)
            block = spreadout[pl.ds(first, steps * pad), :].astype(jnp.bfloat16)

            @pl.when(owner == me)
            def _():
                landed[me] = block

            @pl.when(owner != me)
            def _():
                sendbuf[owner] = block
                sum_copy(owner, me).start()

            return carry

        lax.fori_loop(1, ep_size + 1, send_sums, 0, unroll=True)

    def land_sums(o, carry):
        peer = lax.rem(me + o, peers)
        sum_copy(peer, peer).wait_recv()
        return carry

    lax.fori_loop(1, peers, land_sums, 0, unroll=True)
    total = landed[0].astype(jnp.float32)
    for p in range(1, peers):
        total += landed[p].astype(jnp.float32)
    for t in range(steps):
        at = t * pad
        row = jnp.concatenate([total[at + c : at + c + 1] for c in range(cols)], axis=1)
        out_ref[t : t + 1, :] = row.astype(jnp.bfloat16)

    def sent(o, carry):
        peer = lax.rem(me + o, peers)
        token_copy(peer, me).wait_send()
        sum_copy(peer, me).wait_send()
        return carry

    lax.fori_loop(1, peers, sent, 0, unroll=True)


def with_kernel(tokens, route_experts, route_weight, expert_slot, w_gate, w_up, w_down):
    sub_size = lax.axis_size("sub")
    ep_size = lax.axis_size("ep")
    peers = sub_size * ep_size
    steps, _, part = tokens.shape
    depth, width = w_gate.shape
    cols = part // LANES
    pad = -(-cols // 16) * 16
    block = steps * pad
    bf16, f32 = jnp.bfloat16, jnp.float32
    dma = pltpu.SemaphoreType.DMA

    def body(*refs):
        layer_kernel(peers, sub_size, *refs)

    out = pl.pallas_call(
        body,
        out_shape=jax.ShapeDtypeStruct((steps, part), bf16),
        in_specs=[pl.BlockSpec(memory_space=pl.ANY)] * 7,
        out_specs=pl.BlockSpec(memory_space=pltpu.VMEM),
        scratch_shapes=[
            pltpu.SMEM(expert_slot.shape, jnp.int32),
            pltpu.VMEM((steps, part), bf16),
            pltpu.VMEM(route_experts.shape, jnp.int32),
            pltpu.VMEM(route_weight.shape, f32),
            pltpu.VMEM((block, LANES), f32),
            pltpu.VMEM((block, LANES), bf16),
            pltpu.VMEM((peers, block, LANES), bf16),
            pltpu.VMEM((peers * block, LANES), f32),
            pltpu.VMEM((steps * ep_size, depth), bf16),
            pltpu.VMEM((width // UP_BLOCK, depth, UP_BLOCK), bf16),
            pltpu.VMEM((width // UP_BLOCK, depth, UP_BLOCK), bf16),
            pltpu.VMEM((depth // DOWN_BLOCK, width, DOWN_BLOCK), bf16),
            pltpu.VMEM((steps * ep_size, width), bf16),
            pltpu.VMEM((ep_size * block, LANES), f32),
            pltpu.VMEM((peers, block, LANES), bf16),
            pltpu.VMEM((peers, block, LANES), bf16),
            dma((4,)),
            dma((width // UP_BLOCK,)),
            dma((width // UP_BLOCK,)),
            dma((depth // DOWN_BLOCK,)),
            dma((peers,)),
            dma((peers,)),
            dma((peers,)),
            dma((peers,)),
        ],
        compiler_params=pltpu.CompilerParams(
            collective_id=0, has_side_effects=True, vmem_limit_bytes=56 * 1024 * 1024
        ),
        cost_estimate=pl.CostEstimate(
            flops=6 * steps * ep_size * depth * width,
            bytes_accessed=6 * depth * width,
            transcendentals=steps * ep_size * width,
        ),
    )(expert_slot, tokens.reshape(steps, part), route_experts, route_weight, w_gate, w_up, w_down)
    return out.reshape(steps, 1, part)


def on_device(tokens, route_experts, route_weight, expert_slot, w_gate, w_up, w_down):
    fits = (
        w_gate.shape[1] == FF
        and tokens.shape[1] == 1
        and tokens.shape[2] % DOWN_BLOCK == 0
        and lax.axis_size("ep") == 8
    )
    plan = with_kernel if fits else with_collectives
    return plan(tokens, route_experts, route_weight, expert_slot, w_gate, w_up, w_down)


def solution(mesh):
    return jax.shard_map(
        on_device,
        mesh=mesh,
        in_specs=(
            P(None, ("grp", "ep"), "sub"),
            P(None, "grp", None),
            P(None, "grp", None),
            P(),
            P(None, ("ep", "sub")),
            P(None, ("ep", "sub")),
            P(("ep", "sub"), None),
        ),
        out_specs=P(None, ("grp", "ep"), "sub"),
        check_vma=False,
    )
```

```python
import jax
import jax.numpy as jnp
from jax import lax
from jax.experimental import pallas as pl
from jax.experimental.pallas import tpu as pltpu
from jax.sharding import PartitionSpec as P

FF = 2048
LANES = 128
UP_BLOCK = 1024
DOWN_BLOCK = 1792
MESH = pl.DeviceIdType.MESH


def swiglu(rows, gate_cols, up_cols, down_rows):
    gate = jnp.dot(rows, gate_cols, preferred_element_type=jnp.float32)
    up = jnp.dot(rows, up_cols, preferred_element_type=jnp.float32)
    hidden = (jax.nn.silu(gate) * up).astype(jnp.bfloat16)
    return jnp.dot(hidden, down_rows, preferred_element_type=jnp.float32)


def expert_terms(rows, experts, weights, expert_slot, w_gate, w_up, w_down, first_col):
    labels = jnp.arange(expert_slot.shape[0], dtype=jnp.int32)
    slot = (first_col + 0) // FF
    logical = jnp.sum(jnp.where(expert_slot == slot, labels, 0))
    chosen = experts == logical
    scale = jnp.sum(jnp.where(chosen, weights, 0.0), axis=1)
    total = scale[:, None] * swiglu(rows, w_gate, w_up, w_down)
    return total


def collect(local):
    gathered = lax.all_gather(local, "ep", axis=0, tiled=True)
    return lax.all_gather(gathered, "sub", axis=1, tiled=True)


def spread(total):
    owned = lax.psum_scatter(total, "ep", scatter_dimension=0, tiled=True)
    return lax.psum_scatter(owned, "sub", scatter_dimension=1, tiled=True)


def with_collectives(tokens, route_experts, route_weight, expert_slot, w_gate, w_up, w_down):
    sub_size = lax.axis_size("sub")
    first_col = (lax.axis_index("ep") * sub_size + lax.axis_index("sub")) * w_gate.shape[1]
    steps, count, part = tokens.shape
    rows = jnp.stack([collect(tokens[step]) for step in range(steps)])
    results = []
    for step in range(steps):
        total = expert_terms(
            rows[step],
            route_experts[step],
            route_weight[step],
            expert_slot,
            w_gate,
            w_up,
            w_down,
            first_col,
        )
        results.append(spread(total).astype(jnp.bfloat16))
    return jnp.stack(results)


def layer_kernel(
    peers,
    sub_size,
    slots_ref,
    tokens_ref,
    experts_ref,
    weights_ref,
    gate_ref,
    up_ref,
    down_ref,
    out_ref,
    slots,
    tok,
    exp_in,
    wt_in,
    stage,
    mine,
    gathered,
    wide,
    rows,
    gates,
    ups,
    downs,
    hidden,
    spreadout,
    sendbuf,
    landed,
    small_sem,
    gate_sem,
    up_sem,
    down_sem,
    tok_send,
    tok_recv,
    sum_send,
    sum_recv,
):
    steps, part = tokens_ref.shape
    ep_size = peers // sub_size
    pad = stage.shape[0] // steps
    cols = part // LANES
    n_up = gates.shape[0]
    n_half = part // DOWN_BLOCK
    grp = lax.axis_index("grp")
    my_ep = lax.axis_index("ep")
    my_sub = lax.axis_index("sub")
    me = my_ep * sub_size + my_sub

    barrier = pltpu.get_barrier_semaphore()

    def greet(o, carry):
        peer = lax.rem(me + o, peers)
        pl.semaphore_signal(
            barrier,
            inc=1,
            device_id=(grp, peer // sub_size, lax.rem(peer, sub_size)),
            device_id_type=MESH,
        )
        return carry

    lax.fori_loop(1, peers, greet, 0, unroll=True)

    small = [
        pltpu.make_async_copy(tokens_ref, tok, small_sem.at[0]),
        pltpu.make_async_copy(experts_ref, exp_in, small_sem.at[1]),
        pltpu.make_async_copy(weights_ref, wt_in, small_sem.at[2]),
        pltpu.make_async_copy(slots_ref, slots, small_sem.at[3]),
    ]
    for copy in small:
        copy.start()

    def gate_copy(c):
        at = pl.multiple_of(c * UP_BLOCK, UP_BLOCK)
        return pltpu.make_async_copy(gate_ref.at[:, pl.ds(at, UP_BLOCK)], gates.at[c], gate_sem.at[c])

    def up_copy(c):
        at = pl.multiple_of(c * UP_BLOCK, UP_BLOCK)
        return pltpu.make_async_copy(up_ref.at[:, pl.ds(at, UP_BLOCK)], ups.at[c], up_sem.at[c])

    def down_copy(c):
        at = pl.multiple_of(c * DOWN_BLOCK, DOWN_BLOCK)
        return pltpu.make_async_copy(down_ref.at[:, pl.ds(at, DOWN_BLOCK)], downs.at[c], down_sem.at[c])

    def start_up(c, carry):
        gate_copy(c).start()
        up_copy(c).start()
        return carry

    def start_down(c, carry):
        down_copy(c).start()
        return carry

    lax.fori_loop(0, n_up, start_up, 0, unroll=True)
    lax.fori_loop(0, downs.shape[0], start_down, 0)

    stage[...] = jnp.zeros_like(stage)
    small[0].wait()
    for t in range(steps):
        row = tok[t : t + 1, :].astype(jnp.float32)
        for c in range(cols):
            stage[t * pad + c : t * pad + c + 1, :] = row[:, c * LANES : (c + 1) * LANES]
    mine[...] = stage[...].astype(jnp.bfloat16)
    gathered[me] = mine[...]

    pl.semaphore_wait(barrier, peers - 1)

    def token_copy(peer, slot):
        return pltpu.make_async_remote_copy(
            src_ref=mine,
            dst_ref=gathered.at[slot],
            send_sem=tok_send.at[peer],
            recv_sem=tok_recv.at[slot],
            device_id=(grp, peer // sub_size, lax.rem(peer, sub_size)),
            device_id_type=MESH,
        )

    def send_tokens(o, carry):
        token_copy(lax.rem(me + o, peers), me).start()
        return carry

    lax.fori_loop(1, peers, send_tokens, 0, unroll=True)

    spreadout[...] = jnp.zeros_like(spreadout)
    for copy in small[1:]:
        copy.wait()

    logical = jnp.int32(0)
    for e in range(slots.shape[0]):
        logical += jnp.where(slots[e] == me, jnp.int32(e), jnp.int32(0))
    scales = [
        jnp.sum(
            jnp.where(exp_in[t] == logical, wt_in[t], 0.0), axis=1, keepdims=True
        )
        for t in range(steps)
    ]

    def land_tokens(o, carry):
        peer = lax.rem(me + o, peers)
        token_copy(peer, peer).wait_recv()
        return carry

    lax.fori_loop(1, peers, land_tokens, 0, unroll=True)
    wide[...] = gathered[...].astype(jnp.float32).reshape(wide.shape)
    for s in range(sub_size):
        for c in range(cols):
            picked = [
                wide[pl.ds(s * steps * pad + t * pad + c, ep_size, stride=sub_size * steps * pad), :]
                for t in range(steps)
            ]
            at = s * part + c * LANES
            rows[:, at : at + LANES] = jnp.concatenate(picked, axis=0).astype(jnp.bfloat16)

    def hide(c, carry):
        gate_copy(c).wait()
        up_copy(c).wait()
        gate = jnp.dot(rows[...], gates[c], preferred_element_type=jnp.float32)
        up = jnp.dot(rows[...], ups[c], preferred_element_type=jnp.float32)
        value = gate / (1.0 + jnp.exp(-gate)) * up
        hidden[:, pl.ds(pl.multiple_of(c * UP_BLOCK, UP_BLOCK), UP_BLOCK)] = value.astype(jnp.bfloat16)
        return carry

    lax.fori_loop(0, n_up, hide, 0, unroll=True)

    def tokens_sent(o, carry):
        token_copy(lax.rem(me + o, peers), me).wait_send()
        return carry

    lax.fori_loop(1, peers, tokens_sent, 0, unroll=True)

    def sum_copy(owner, slot):
        return pltpu.make_async_remote_copy(
            src_ref=sendbuf.at[owner],
            dst_ref=landed.at[slot],
            send_sem=sum_send.at[owner],
            recv_sem=sum_recv.at[slot],
            device_id=(grp, owner // sub_size, lax.rem(owner, sub_size)),
            device_id_type=MESH,
        )

    for s in range(sub_size):

        def lower(n, carry):
            down_copy(s * n_half + n).wait()
            value = jnp.dot(hidden[...], downs[s * n_half + n], preferred_element_type=jnp.float32)
            for t in range(steps):
                term = value[t * ep_size : (t + 1) * ep_size] * scales[t]
                for k in range(DOWN_BLOCK // LANES):
                    start = t * pad + n * (DOWN_BLOCK // LANES) + k
                    spreadout[pl.ds(start, ep_size, stride=steps * pad), :] = term[
                        :, k * LANES : (k + 1) * LANES
                    ]
            return carry

        lax.fori_loop(0, n_half, lower, 0)

        def send_sums(o, carry):
            j = lax.rem(my_ep + o, ep_size)
            owner = j * sub_size + s
            first = pl.multiple_of(j * steps * pad, steps * pad)
            block = spreadout[pl.ds(first, steps * pad), :].astype(jnp.bfloat16)

            @pl.when(owner == me)
            def _():
                landed[me] = block

            @pl.when(owner != me)
            def _():
                sendbuf[owner] = block
                sum_copy(owner, me).start()

            return carry

        lax.fori_loop(1, ep_size + 1, send_sums, 0, unroll=True)

    def land_sums(o, carry):
        peer = lax.rem(me + o, peers)
        sum_copy(peer, peer).wait_recv()
        return carry

    lax.fori_loop(1, peers, land_sums, 0, unroll=True)
    total = landed[0].astype(jnp.float32)
    for p in range(1, peers):
        total += landed[p].astype(jnp.float32)
    for t in range(steps):
        at = t * pad
        row = jnp.concatenate([total[at + c : at + c + 1] for c in range(cols)], axis=1)
        tok[t : t + 1, :] = row.astype(jnp.bfloat16)
    result = pltpu.make_async_copy(tok, out_ref, small_sem.at[0])
    result.start()

    def sent(o, carry):
        peer = lax.rem(me + o, peers)
        sum_copy(peer, me).wait_send()
        return carry

    lax.fori_loop(1, peers, sent, 0, unroll=True)
    result.wait()


def with_kernel(tokens, route_experts, route_weight, expert_slot, w_gate, w_up, w_down):
    sub_size = lax.axis_size("sub")
    ep_size = lax.axis_size("ep")
    peers = sub_size * ep_size
    steps, _, part = tokens.shape
    depth, width = w_gate.shape
    cols = part // LANES
    pad = -(-cols // 16) * 16
    block = steps * pad
    bf16, f32 = jnp.bfloat16, jnp.float32
    dma = pltpu.SemaphoreType.DMA

    def body(*refs):
        layer_kernel(peers, sub_size, *refs)

    out = pl.pallas_call(
        body,
        out_shape=jax.ShapeDtypeStruct((steps, part), bf16),
        in_specs=[pl.BlockSpec(memory_space=pl.ANY)] * 7,
        out_specs=pl.BlockSpec(memory_space=pl.ANY),
        scratch_shapes=[
            pltpu.SMEM(expert_slot.shape, jnp.int32),
            pltpu.VMEM((steps, part), bf16),
            pltpu.VMEM(route_experts.shape, jnp.int32),
            pltpu.VMEM(route_weight.shape, f32),
            pltpu.VMEM((block, LANES), f32),
            pltpu.VMEM((block, LANES), bf16),
            pltpu.VMEM((peers, block, LANES), bf16),
            pltpu.VMEM((peers * block, LANES), f32),
            pltpu.VMEM((steps * ep_size, depth), bf16),
            pltpu.VMEM((width // UP_BLOCK, depth, UP_BLOCK), bf16),
            pltpu.VMEM((width // UP_BLOCK, depth, UP_BLOCK), bf16),
            pltpu.VMEM((depth // DOWN_BLOCK, width, DOWN_BLOCK), bf16),
            pltpu.VMEM((steps * ep_size, width), bf16),
            pltpu.VMEM((ep_size * block, LANES), f32),
            pltpu.VMEM((peers, block, LANES), bf16),
            pltpu.VMEM((peers, block, LANES), bf16),
            dma((4,)),
            dma((width // UP_BLOCK,)),
            dma((width // UP_BLOCK,)),
            dma((depth // DOWN_BLOCK,)),
            dma((peers,)),
            dma((peers,)),
            dma((peers,)),
            dma((peers,)),
        ],
        compiler_params=pltpu.CompilerParams(
            collective_id=0, has_side_effects=True, vmem_limit_bytes=56 * 1024 * 1024
        ),
        cost_estimate=pl.CostEstimate(
            flops=6 * steps * ep_size * depth * width,
            bytes_accessed=6 * depth * width,
            transcendentals=steps * ep_size * width,
        ),
    )(expert_slot, tokens.reshape(steps, part), route_experts, route_weight, w_gate, w_up, w_down)
    return out.reshape(steps, 1, part)


def on_device(tokens, route_experts, route_weight, expert_slot, w_gate, w_up, w_down):
    fits = (
        w_gate.shape[1] == FF
        and tokens.shape[1] == 1
        and tokens.shape[2] % DOWN_BLOCK == 0
        and lax.axis_size("ep") == 8
    )
    plan = with_kernel if fits else with_collectives
    return plan(tokens, route_experts, route_weight, expert_slot, w_gate, w_up, w_down)


def solution(mesh):
    return jax.shard_map(
        on_device,
        mesh=mesh,
        in_specs=(
            P(None, ("grp", "ep"), "sub"),
            P(None, "grp", None),
            P(None, "grp", None),
            P(),
            P(None, ("ep", "sub")),
            P(None, ("ep", "sub")),
            P(("ep", "sub"), None),
        ),
        out_specs=P(None, ("grp", "ep"), "sub"),
        check_vma=False,
    )
```
